512 devices in a mesh: section: 16 (over y, z_hi, core), expert: 32 (over z_lo, x).
Axes of the slice: x: 4, y: 4, z: 16 (z_hi: 2, z_lo: 8; z = z_hi * 8 + z_lo), core: 2. Of those that a mesh axis runs over, the one named last changes fastest.
Arguments:
- cotangent: bfloat16 [16, 2, 2048, 3584], P('section', None, 'expert'), may hold values from -6 to 6
- routes: int32 [16, 2, 2048, 1], P('section', None, 'expert'), may hold values from 0 to 3; in each aligned block of 64 rows (0 to 63, 64 to 127, ..., all dimensions but the last counted through in order) at most 17 rows name the same one
- gate_prob: float32 [16, 2, 2048, 1], P('section', None, 'expert'), may hold values from 0.5 to 1.5
- saved_gate: bfloat16 [16, 2, 32, 17, 4096], P('section', None, None, None, 'expert'), may hold values from -6 to 6
- saved_up: bfloat16 [16, 2, 32, 17, 4096], P('section', None, None, None, 'expert'), may hold values from -6 to 6
- w_gate: bfloat16 [16, 3584, 4096], P('section', None, 'expert'), may hold values from -0.1875 to 0.1875
- w_up: bfloat16 [16, 3584, 4096], P('section', None, 'expert'), may hold values from -0.1875 to 0.1875
- w_down: bfloat16 [16, 4096, 3584], P('section', 'expert'), may hold values from -0.09375 to 0.09375
Outputs:
- input_grads: bfloat16 [16, 2, 2048, 3584], P('section', None, 'expert')
- gate_grads: float32 [16, 2, 2048, 1], P('section', None, 'expert')
The draws below stay inside these ranges and needn't reach their ends.
Inputs may be any that keep to these rules, and one draw needn't show every extreme that they name: `routes`: among one index's 64 tokens of one micro-batch at most 17 choose the same expert.
All inputs are finite; a program needn't handle non-finite values.
Results may differ from the reference program's by a relative error of at most 0.01.
Values may be sent and summed in bfloat16 or wider, within the bound.
A program may use at most 128 MiB of HBM per device.

```python
import math
import jax
import jax.numpy as jnp
import numpy as np
from jax import lax

D = 3584
FF = 1024
EXPERTS = 4
TOP = 1
MB = 2
TOK = 64
CAP = 17
SECTIONS = 16
TOKENS = 2048
GROUP = 8
FH = 128
HID = 4096
N_EXPERT = 32


def steps_of(rng, dims, split, least, high):
    def one(axis_at, blocks):
        heights = jax.random.uniform(jax.random.fold_in(jax.random.fold_in(rng, 6), axis_at), (blocks,), jnp.float32, least / len(split), high / len(split))
        return jnp.repeat(jnp.exp(heights), dims[axis_at] // blocks).reshape((-1,) + (1,) * (len(dims) - axis_at - 1))

    loudness = one(*split[0])
    for cut in split[1:]:
        loudness = loudness * one(*cut)
    return loudness


def routed_block(stream_key, own, number, rows, count, top, bound, skew):
    ranking = jax.random.permutation(stream_key, count)
    crowded, ordinary = load_shares(count, rows * top, bound, skew, True), load_shares(count, rows * top, bound, skew, False)
    places = jnp.arange(count)

    def named(sizes, rotation):
        used = int((sizes > 0).sum())
        fixed = max(1, used // 4)
        moved = fixed + (places - fixed + rotation * (used - fixed)) % max(1, count - fixed)
        return jnp.zeros((count,), jnp.int32).at[ranking[jnp.where(places < fixed, places, moved)]].set(jnp.asarray(sizes, jnp.int32))

    sizes = jnp.where(number % 4 == 0, named(crowded, number // 4), named(ordinary, number - number // 4 - 1))
    mixed = jax.random.permutation(jax.random.fold_in(own, 3), count)
    giver, receiver = mixed[0:count // 2 * 2:2], mixed[1:count // 2 * 2:2]
    margin = jnp.minimum(sizes[giver] - 1, bound - sizes[receiver]) // 2
    margin = jnp.where((giver == ranking[0]) | (receiver == ranking[0]) | (sizes[receiver] == 0), 0, jnp.maximum(margin, 0))
    moved = jax.random.randint(jax.random.fold_in(own, 4), (count // 2,), 0, 1 << 20) % (margin + 1)
    sizes = sizes.at[giver].add(-moved).at[receiver].add(moved)
    members = jnp.searchsorted(jnp.cumsum(sizes), jnp.arange(rows * top), side="right").astype(jnp.int32)
    grid = members.reshape(top, rows).T
    grid = grid[jax.random.permutation(jax.random.fold_in(own, 1), rows)]
    rotation = jax.random.randint(jax.random.fold_in(own, 2), (rows, 1), 0, top)
    return jnp.take_along_axis(grid, (jnp.arange(top)[None, :] + rotation) % top, axis=1)


def load_shares(count, total, bound, skew, full):
    loads = [(1 << 20) // math.isqrt(grade ** skew) + 1 for grade in range(1, count + 1)]
    largest = bound if full else min(bound, max(-(-total // count), total * loads[0] // sum(loads)))
    least = 1 if total - largest >= count - 1 else 0
    counts, surplus = [largest] + [least] * (count - 1), total - largest - least * (count - 1)
    while surplus > 0:
        free = [i for i in range(1, count) if counts[i] < largest] or [i for i in range(1, count) if counts[i] < bound]
        pool, remaining = sum([loads[i] for i in free]), surplus
        for i in free:
            addition = min(bound - counts[i], max(1, remaining * loads[i] // pool), surplus)
            counts[i] = counts[i] + addition
            surplus = surplus - addition
    return np.array(counts)


def scatter_about(rng, shape, scale, reach, cuts=(), kind=jnp.bfloat16):
    entries = scale * jax.random.normal(rng, shape, jnp.float32)
    if cuts:
        entries = entries * steps_of(rng, shape, cuts, -0.22, 0.18)
    return jnp.clip(entries, -reach, reach).astype(kind)


def setup_inputs(seed: int = 0) -> dict:
    seeds = jax.random.split(jax.random.key(seed), 9)
    cotangent = scatter_about(seeds[0], (SECTIONS, MB, TOKENS, D), 1.0, 6.0, ((0, 16), (2, 32)))
    routes_keys = jax.random.split(jax.random.fold_in(seeds[1], 1), SECTIONS * MB * TOKENS // TOK)
    routes_turns = jax.random.permutation(jax.random.fold_in(seeds[1], 3), SECTIONS * MB * TOKENS // TOK)
    routes = jax.vmap(lambda own, number: routed_block(jax.random.fold_in(seeds[1], 2), own, number, TOK, EXPERTS, TOP, CAP, 2))(routes_keys, routes_turns).reshape((SECTIONS, MB, TOKENS, TOP))
    gate_prob = jnp.clip(0.5 + 1.0 * jax.random.uniform(seeds[2], (SECTIONS, MB, TOKENS, TOP), jnp.float32) ** steps_of(seeds[2], (SECTIONS, MB, TOKENS, TOP), ((0, 16), (2, 32)), -0.2, 0.2), 0.5, 1.5)
    saved_gate = scatter_about(seeds[3], (SECTIONS, MB, N_EXPERT, CAP, HID), 1.5, 6.0, ((0, 16), (4, 32)))
    saved_up = scatter_about(seeds[4], (SECTIONS, MB, N_EXPERT, CAP, HID), 1.0, 6.0, ((0, 16), (4, 32)))
    w_gate = scatter_about(seeds[5], (SECTIONS, D, HID), FF ** -0.5, 0.1875, ((0, 16), (2, 32)))
    w_up = scatter_about(seeds[6], (SECTIONS, D, HID), FF ** -0.5, 0.1875, ((0, 16), (2, 32)))
    w_down = scatter_about(seeds[7], (SECTIONS, HID, D), D ** -0.5, 0.09375, ((0, 16), (1, 32)))
    return dict(cotangent=cotangent, routes=routes, gate_prob=gate_prob, saved_gate=saved_gate, saved_up=saved_up, w_gate=w_gate, w_up=w_up, w_down=w_down)


def section_backward(incoming, expert_ids, prob, pre_gate, pre_up, weight_gate, weight_up, weight_down):
    sources = N_EXPERT
    ids_block = expert_ids.reshape(sources, TOK)
    onehot = (ids_block[..., None] == jnp.arange(EXPERTS, dtype=jnp.int32)[None, None, :]).astype(jnp.int32)
    ranks = jnp.sum((jnp.cumsum(onehot, axis=1) - 1) * onehot, axis=2)
    row_position = (jnp.arange(sources, dtype=jnp.int32)[:, None] * CAP + ranks).reshape(-1).astype(jnp.int32)
    buffers = jnp.zeros((EXPERTS, sources * CAP, D), jnp.bfloat16).at[expert_ids, row_position].set(incoming)
    flat_rows = sources * CAP
    expert_parts = []
    score_parts = []
    for which in range(EXPERTS):
        routed_rows = buffers[which]
        lower_col = which * FF
        grad_hidden = jnp.dot(routed_rows, weight_down[lower_col:lower_col + FF].T, preferred_element_type=jnp.float32)
        gate_val = pre_gate[:, :, lower_col:lower_col + FF].reshape(flat_rows, FF).astype(jnp.float32)
        up_val = pre_up[:, :, lower_col:lower_col + FF].reshape(flat_rows, FF).astype(jnp.float32)
        sigmoid_gate = 1.0 / (1.0 + jnp.exp(-gate_val))
        silu_gate = gate_val * sigmoid_gate
        score_block = jnp.sum((silu_gate * up_val * grad_hidden).reshape(flat_rows, GROUP, FH), axis=2).astype(jnp.bfloat16)
        score_block = lax.optimization_barrier(score_block)
        score_parts.append(jnp.sum(score_block.astype(jnp.float32), axis=1))
        grad_up = (grad_hidden * silu_gate).astype(jnp.bfloat16)
        grad_gate = (grad_hidden * up_val * sigmoid_gate * (1.0 + gate_val * (1.0 - sigmoid_gate))).astype(jnp.bfloat16)
        gate_cols = weight_gate[:, lower_col:lower_col + FF].reshape(D, GROUP, FH).astype(jnp.float32)
        up_cols = weight_up[:, lower_col:lower_col + FF].reshape(D, GROUP, FH).astype(jnp.float32)
        partial_value = jnp.einsum('rjf,djf->rjd', grad_gate.reshape(flat_rows, GROUP, FH).astype(jnp.float32), gate_cols)
        partial_value = partial_value + jnp.einsum('rjf,djf->rjd', grad_up.reshape(flat_rows, GROUP, FH).astype(jnp.float32), up_cols)
        partial_value = lax.optimization_barrier(partial_value.astype(jnp.bfloat16))
        expert_parts.append(jnp.sum(partial_value.astype(jnp.float32), axis=1))
    all_parts = jnp.stack(expert_parts, axis=0)
    all_scores = jnp.stack(score_parts, axis=0)
    token_part = all_parts[expert_ids, row_position]
    token_score = all_scores[expert_ids, row_position]
    result = (incoming.astype(jnp.float32) + prob[:, None] * token_part).astype(jnp.bfloat16)
    return result, token_score


def per_section(stacked):
    cotangent, routes, gate_prob, saved_gate, saved_up, w_gate, w_up, w_down = stacked
    grads_list = []
    score_list = []
    for microbatch in range(MB):
        result, score = section_backward(cotangent[microbatch], routes[microbatch, :, 0], gate_prob[microbatch, :, 0], saved_gate[microbatch], saved_up[microbatch], w_gate, w_up, w_down)
        grads_list.append(result)
        score_list.append(score)
    return jnp.stack(grads_list, axis=0), jnp.stack(score_list, axis=0)


def reference(cotangent, routes, gate_prob, saved_gate, saved_up, w_gate, w_up, w_down):
    grads_all, scores_all = lax.map(per_section, (cotangent, routes, gate_prob, saved_gate, saved_up, w_gate, w_up, w_down))
    shifted = jnp.concatenate([grads_all[1:, 0], jnp.zeros_like(grads_all[:1, 0])], axis=0)
    input_grads = grads_all.at[:, 0].set(shifted)
    return input_grads, scores_all[..., None]
```

```python
import jax
import jax.numpy as jnp
from jax import lax
from jax.experimental import pallas as pl
from jax.experimental.pallas import tpu as pltpu
from jax.sharding import PartitionSpec as P

MESH = pl.DeviceIdType.MESH
BF16 = jnp.bfloat16
F32 = jnp.float32

TOK = 64
D = 3584
X = 4
Z = 8
EXPERTS = 4
SLICE = D // X
CHUNKS = SLICE // 128
TILE = 16
WIDE = SLICE + 128
SOURCES = X * Z
MAIN = SOURCES * TILE
ROWS = MAIN + SOURCES
FH = 128
BAND = X * TILE
SCORE_ROW = 8


def dot(a, b):
    return lax.dot_general(a, b, (((1,), (0,)), ((), ())), preferred_element_type=F32)


def dot_t(a, b):
    return lax.dot_general(a, b, (((1,), (1,)), ((), ())), preferred_element_type=F32)


def iota(shape, axis):
    return lax.broadcasted_iota(jnp.int32, shape, axis)


def waited(ref, sem):
    pltpu.make_async_copy(ref, ref, sem).wait()


def kernel(
    ids_col, ids_row, prob, cot, saved_gate, saved_up, w_gate, w_up, w_down,
    out, scores,
    sent, routed, wd, wg, wu, a_sent, a_got, hidden, part, mate_part, total, back, handed,
    send_sem, routed_sem, relay_sem, w_send, w_sem, w_own, a_send, a_sem, h_send, h_sem,
    mate_send, mate_sem, total_send, back_sem, hand_send, hand_sem,
):
    sec = lax.axis_index("section")
    me = lax.axis_index("expert")
    sections = lax.axis_size("section")
    z, x = me // X, me % X
    expert, side = z // 2, z % 2
    mate = z + 1 - 2 * side
    mate_id = mate * X + x
    owned = jnp.where(side == 0, z + 1, Z - z)
    others = jnp.where(side == 0, Z - mate, mate + 1)
    away = jnp.where(side == 0, -1, 1)

    def at(index):
        return dict(device_id={"expert": index}, device_id_type=MESH)

    def band(plane):
        return pl.ds(pl.multiple_of(plane * BAND, BAND), BAND)

    def rows16(index):
        return pl.ds(pl.multiple_of(index * TILE, TILE), TILE)

    barrier = pltpu.get_barrier_semaphore()

    def greet(step, carry):
        pl.semaphore_signal(barrier, inc=1, **at((me + step) % (X * Z)))
        return carry

    lax.fori_loop(1, X * Z, greet, 0)

    @pl.when(sec > 0)
    def _():
        pl.semaphore_signal(barrier, inc=1, device_id={"section": sec - 1}, device_id_type=MESH)

    @pl.when(sec < sections - 1)
    def _():
        pl.semaphore_signal(barrier, inc=1, device_id={"section": sec + 1}, device_id_type=MESH)

    ends = jnp.where(sec > 0, 1, 0) + jnp.where(sec < sections - 1, 1, 0)

    def pack(mb):
        ids = ids_row[mb]
        hot = (iota((8, TOK), 0) == ids).astype(F32)
        before = (iota((TOK, TOK), 0) < iota((TOK, TOK), 1)).astype(BF16)
        rank = jnp.sum(dot(hot.astype(BF16), before) * hot, axis=0, keepdims=True).astype(jnp.int32)
        row = iota((2 * TOK, TOK), 0)
        main = jnp.logical_and(row == ids * TILE + rank, jnp.logical_and(rank < TILE, row < TOK))
        last = jnp.logical_and((row - TOK) // TILE == ids, jnp.logical_and(rank == TILE, row >= TOK))
        pick = jnp.logical_or(main, last).astype(BF16)
        place = iota((TOK, 128), 0) % TILE
        for d in range(X):
            picked = dot(pick, cot[mb, :, d * SLICE : (d + 1) * SLICE])
            sent[mb, d, :, 0:SLICE] = picked[0:TOK].astype(BF16)
            folded = jnp.zeros((TOK, 128), F32)
            for k in range(CHUNKS):
                folded = jnp.where(place == k, picked[TOK:, k * 128 : (k + 1) * 128], folded)
            sent[mb, d, :, SLICE:WIDE] = folded.astype(BF16)

    def dispatch(mb):
        def one(step, carry):
            far = step // X
            e = jnp.where(z < Z // 2, EXPERTS - 1 - far, far)
            d = (x + 1 + step) % X
            near = jnp.where(z <= 2 * e, 2 * e, 2 * e + 1)
            target = near * X + d
            src = sent.at[mb, d, rows16(e), :]
            dst = routed.at[mb, rows16(me), :]

            @pl.when(target == me)
            def _():
                pltpu.make_async_copy(src, dst, routed_sem.at[mb, z]).start()

            @pl.when(target != me)
            def _():
                pltpu.make_async_remote_copy(
                    src, dst, send_sem.at[mb], routed_sem.at[mb, z], **at(target)
                ).start()

            return carry

        lax.fori_loop(0, X * EXPERTS, one, 0)

    def relay(mb, first, last):
        def one(step, carry):
            plane = z + away * step
            block = routed.at[mb, band(plane), :]
            waited(block, routed_sem.at[mb, plane])
            pltpu.make_async_remote_copy(
                block, block, relay_sem.at[mb, plane], routed_sem.at[mb, plane], **at(mate_id)
            ).start()
            return carry

        lax.fori_loop(first, last, one, 0)

    def arrivals(mb):
        def one(step, carry):
            plane = mate - away * step
            waited(routed.at[mb, band(plane), :], routed_sem.at[mb, plane])
            return carry

        lax.fori_loop(0, others, one, 0)

    def weights():
        for j in range(X):
            d = (x + j) % X
            across = pl.ds(pl.multiple_of(d * SLICE, 128), SLICE)
            pairs = (
                (w_down.at[:, across], wd.at[j]),
                (w_gate.at[across, :], wg.at[j]),
                (w_up.at[across, :], wu.at[j]),
            )
            for which, (src, dst) in enumerate(pairs):
                if j == 0:
                    pltpu.make_async_copy(src, dst, w_own.at[which]).start()
                else:
                    pltpu.make_async_remote_copy(
                        src, dst, w_send.at[which, j - 1], w_sem.at[which, j - 1], **at(z * X + d)
                    ).start()

    def weights_here(which, ref):
        waited(ref.at[0], w_own.at[which])
        for j in range(1, X):
            waited(ref.at[j], w_sem.at[which, j - 1])

    def first_product(mb):
        row = iota((CHUNKS * SOURCES, MAIN), 0)
        unfold = (iota((CHUNKS * SOURCES, MAIN), 1) == (row % SOURCES) * TILE + row // SOURCES).astype(BF16)
        tail = dot(unfold, routed[mb, :, SLICE:WIDE]).astype(BF16)
        tail = jnp.concatenate(
            [tail[k * SOURCES : (k + 1) * SOURCES] for k in range(CHUNKS)], axis=1
        )
        for j in range(X):
            a_sent[mb, j, 0:MAIN] = dot_t(routed[mb, :, 0:SLICE], wd[j]).astype(BF16)
            a_sent[mb, j, MAIN:ROWS] = dot_t(tail, wd[j]).astype(BF16)
        for j in range(1, X):
            pltpu.make_async_remote_copy(
                a_sent.at[mb, j], a_got.at[mb, j - 1], a_send.at[mb, j - 1], a_sem.at[mb, j - 1],
                **at(z * X + (x + X - j) % X),
            ).start()

    def activate(mb):
        for j in range(1, X):
            waited(a_got.at[mb, j - 1], a_sem.at[mb, j - 1])
        a = a_sent[mb, 0].astype(F32)
        for j in range(1, X):
            a = a + a_got[mb, j - 1].astype(F32)
        g = saved_gate[mb].astype(F32)
        u = saved_up[mb].astype(F32)
        sg = 1.0 / (1.0 + jnp.exp(-g))
        grad_up = a * (g * sg)
        grad_gate = a * u * sg * (1.0 + g * (1.0 - sg))
        hidden[mb, 0, :, 0:FH] = grad_gate.astype(BF16)
        hidden[mb, 0, :, FH : 2 * FH] = grad_up.astype(BF16)
        for j in range(1, X):
            pltpu.make_async_remote_copy(
                hidden.at[mb, 0], hidden.at[mb, j], h_send.at[mb, j - 1], h_sem.at[mb, j - 1],
                **at(z * X + (x + j) % X),
            ).start()
        score = jnp.sum(grad_up * u, axis=1, keepdims=True)
        row = iota((ROWS, 128), 0)
        slot = jnp.where(row < MAIN, row % TILE, TILE)
        spread = jnp.where(iota((ROWS, 128), 1) == slot, score, 0.0).astype(BF16)
        row, other = iota((MAIN, ROWS), 0), iota((MAIN, ROWS), 1)
        source = jnp.where(other < MAIN, other // TILE, other - MAIN)
        gather = jnp.logical_and(row % TILE == SCORE_ROW, row // TILE == source).astype(BF16)
        part[mb, :, SLICE:WIDE] = dot(gather, spread).astype(BF16)

    def second_product(mb):
        for j in range(1, X):
            waited(hidden.at[mb, j], h_sem.at[mb, j - 1])
        grads = jnp.zeros((ROWS, SLICE), F32)
        for j in range(X):
            both = jnp.concatenate([wg[j], wu[j]], axis=1)
            grads = grads + dot_t(hidden[mb, j], both)
        part[mb, :, 0:SLICE] = grads[0:MAIN].astype(BF16)
        tail = grads[MAIN:ROWS].astype(BF16)
        spread = dot((iota((MAIN, SOURCES), 0) // TILE == iota((MAIN, SOURCES), 1)).astype(BF16), tail)
        place = iota((MAIN, 128), 0) % TILE
        folded = part[mb, :, SLICE:WIDE].astype(F32)
        for k in range(CHUNKS):
            folded = jnp.where(place == k, spread[:, k * 128 : (k + 1) * 128], folded)
        part[mb, :, SLICE:WIDE] = folded.astype(BF16)

        def one(step, carry):
            plane = mate - away * step
            pltpu.make_async_remote_copy(
                part.at[mb, band(plane), :], mate_part.at[mb, band(plane), :],
                mate_send.at[mb, plane], mate_sem.at[mb, plane], **at(mate_id),
            ).start()
            return carry

        lax.fori_loop(0, others, one, 0)

    def send_back(mb):
        def one(step, carry):
            plane = z + away * (owned - 1 - step)
            rows = band(plane)
            waited(mate_part.at[mb, rows, :], mate_sem.at[mb, plane])
            both = part[mb, rows, :].astype(F32) + mate_part[mb, rows, :].astype(F32)
            total[mb, rows, :] = both.astype(BF16)

            def to(step, carry):
                target = plane * X + (x + 1 + step) % X
                src = total.at[mb, rows16(target), :]
                dst = back.at[mb, x, rows16(expert), :]

                @pl.when(target == me)
                def _():
                    pltpu.make_async_copy(src, dst, back_sem.at[mb]).start()

                @pl.when(target != me)
                def _():
                    pltpu.make_async_remote_copy(
                        src, dst, total_send.at[mb, plane], back_sem.at[mb], **at(target)
                    ).start()

                return carry

            lax.fori_loop(0, X, to, 0)
            return carry

        lax.fori_loop(0, owned, one, 0)

    def finish(mb):
        waited(back.at[mb], back_sem.at[mb])
        ids = ids_col[mb]
        lane = iota((TOK, 128), 1)
        hot = (lane == ids).astype(F32)
        before = (iota((TOK, TOK), 1) < iota((TOK, TOK), 0)).astype(BF16)
        rank = jnp.sum(dot(before, hot.astype(BF16)) * hot, axis=1, keepdims=True).astype(jnp.int32)
        column = iota((TOK, TOK), 1)
        main = jnp.logical_and(column == ids * TILE + rank, rank < TILE).astype(BF16)
        group = [
            jnp.logical_and(column == ids * TILE + k, rank == TILE).astype(F32) for k in range(CHUNKS)
        ]
        group.append((column == ids * TILE + SCORE_ROW).astype(F32))
        pick = jnp.concatenate(group, axis=0).astype(BF16)
        score = jnp.zeros((TOK, 128), F32)
        weight = prob[mb]
        for d in range(X):
            tail = dot(pick, back[mb, d, :, SLICE:WIDE])
            score = score + tail[CHUNKS * TOK :]
            grads = dot(main, back[mb, d, :, 0:SLICE])
            grads = grads + jnp.concatenate(
                [tail[k * TOK : (k + 1) * TOK] for k in range(CHUNKS)], axis=1
            )
            across = slice(d * SLICE, (d + 1) * SLICE)
            dx = (cot[mb, :, across].astype(F32) + weight * grads).astype(BF16)
            if mb == 0:
                handed[:, across] = dx
            else:
                out[mb, :, across] = dx
        scores[mb] = jnp.sum(jnp.where(lane == rank, score, 0.0), axis=1, keepdims=True)

    pack(0)
    pl.semaphore_wait(barrier, X * Z - 1 + ends)
    dispatch(0)
    weights()
    pack(1)
    dispatch(1)
    relay(0, 0, owned)
    arrivals(0)
    weights_here(0, wd)
    first_product(0)
    half = (owned + 1) // 2
    relay(1, 0, half)
    activate(0)
    relay(1, half, owned)
    arrivals(1)
    first_product(1)
    weights_here(1, wg)
    weights_here(2, wu)
    second_product(0)
    activate(1)
    send_back(0)
    second_product(1)
    send_back(1)
    finish(0)

    @pl.when(sec > 0)
    def _():
        pltpu.make_async_remote_copy(
            handed, out.at[0], hand_send, hand_sem, device_id={"section": sec - 1}, device_id_type=MESH
        ).start()

    @pl.when(sec == sections - 1)
    def _():
        out[0] = jnp.zeros((TOK, D), BF16)

    finish(1)

    for mb in range(2):
        waited(routed.at[mb, pl.ds(0, (X * EXPERTS - 1) * TILE), :], send_sem.at[mb])

        def relayed(step, carry):
            plane = z + away * step
            waited(routed.at[mb, band(plane), :], relay_sem.at[mb, plane])
            rows = total.at[mb, band(plane), :]

            @pl.when(plane == z)
            def _():
                waited(total.at[mb, pl.ds(0, BAND - TILE), :], total_send.at[mb, plane])

            @pl.when(plane != z)
            def _():
                waited(rows, total_send.at[mb, plane])

            return carry

        lax.fori_loop(0, owned, relayed, 0)

        def mated(step, carry):
            plane = mate - away * step
            waited(part.at[mb, band(plane), :], mate_send.at[mb, plane])
            return carry

        lax.fori_loop(0, others, mated, 0)
        for j in range(1, X):
            waited(a_sent.at[mb, j], a_send.at[mb, j - 1])
            waited(hidden.at[mb, 0], h_send.at[mb, j - 1])
    for which, ref in enumerate((wd, wg, wu)):
        for j in range(1, X):
            waited(ref.at[j], w_send.at[which, j - 1])

    @pl.when(sec > 0)
    def _():
        waited(handed, hand_send)

    @pl.when(sec < sections - 1)
    def _():
        waited(out.at[0], hand_sem)


def on_device(cotangent, routes, gate_prob, saved_gate, saved_up, w_gate, w_up, w_down):
    def by_row(saved):
        main = saved[0, :, :, :TILE, :].reshape(2, MAIN, FH)
        return jnp.concatenate([main, saved[0, :, :, TILE, :]], axis=1)

    vmem = pl.BlockSpec(memory_space=pltpu.VMEM)
    hbm = pl.BlockSpec(memory_space=pl.ANY)
    dma = pltpu.SemaphoreType.DMA
    grads, scores = pl.pallas_call(
        kernel,
        out_shape=(
            jax.ShapeDtypeStruct((2, TOK, D), BF16),
            jax.ShapeDtypeStruct((2, TOK, 1), F32),
        ),
        in_specs=[vmem] * 6 + [hbm] * 3,
        out_specs=(vmem, vmem),
        scratch_shapes=[
            pltpu.VMEM((2, X, TOK, WIDE), BF16),
            pltpu.VMEM((2, MAIN, WIDE), BF16),
            pltpu.VMEM((X, FH, SLICE), BF16),
            pltpu.VMEM((X, SLICE, FH), BF16),
            pltpu.VMEM((X, SLICE, FH), BF16),
            pltpu.VMEM((2, X, ROWS, FH), BF16),
            pltpu.VMEM((2, X - 1, ROWS, FH), BF16),
            pltpu.VMEM((2, X, ROWS, 2 * FH), BF16),
            pltpu.VMEM((2, MAIN, WIDE), BF16),
            pltpu.VMEM((2, MAIN, WIDE), BF16),
            pltpu.VMEM((2, MAIN, WIDE), BF16),
            pltpu.VMEM((2, X, TOK, WIDE), BF16),
            pltpu.VMEM((TOK, D), BF16),
            dma((2,)),
            dma((2, Z)),
            dma((2, Z)),
            dma((3, X - 1)),
            dma((3, X - 1)),
            dma((3,)),
            dma((2, X - 1)),
            dma((2, X - 1)),
            dma((2, X - 1)),
            dma((2, X - 1)),
            dma((2, Z)),
            dma((2, Z)),
            dma((2, Z)),
            dma((2,)),
            dma,
            dma,
        ],
        compiler_params=pltpu.CompilerParams(
            collective_id=0, has_side_effects=True, vmem_limit_bytes=48 * 1024 * 1024
        ),
        cost_estimate=pl.CostEstimate(
            flops=6 * 2 * ROWS * D * FH, bytes_accessed=8 * 1024 * 1024, transcendentals=2 * ROWS * FH
        ),
    )(
        routes[0],
        routes[0].reshape(2, 1, TOK),
        gate_prob[0],
        cotangent[0],
        by_row(saved_gate),
        by_row(saved_up),
        w_gate[0],
        w_up[0],
        w_down[0],
    )
    return grads[None], scores[None]


def solution(mesh):
    in_specs = (
        P("section", None, "expert", None),
        P("section", None, "expert", None),
        P("section", None, "expert", None),
        P("section", None, None, None, "expert"),
        P("section", None, None, None, "expert"),
        P("section", None, "expert"),
        P("section", None, "expert"),
        P("section", "expert", None),
    )
    out_specs = (P("section", None, "expert", None), P("section", None, "expert", None))
    return jax.shard_map(
        on_device, mesh=mesh, in_specs=in_specs, out_specs=out_specs, check_vma=False
    )
```

```python
import jax
import jax.numpy as jnp
from jax import lax
from jax.experimental import pallas as pl
from jax.experimental.pallas import tpu as pltpu
from jax.sharding import PartitionSpec as P

MESH = pl.DeviceIdType.MESH
BF16 = jnp.bfloat16
F32 = jnp.float32

TOK = 64
D = 3584
X = 4
Z = 8
EXPERTS = 4
SLICE = D // X
CHUNKS = SLICE // 128
TILE = 16
WIDE = SLICE + 128
SOURCES = X * Z
MAIN = SOURCES * TILE
ROWS = MAIN + SOURCES
FH = 128
BAND = X * TILE
VMEM_MB = 28
SCORE_ROW = 8


def dot(a, b):
    return lax.dot_general(a, b, (((1,), (0,)), ((), ())), preferred_element_type=F32)


def dot_t(a, b):
    return lax.dot_general(a, b, (((1,), (1,)), ((), ())), preferred_element_type=F32)


def iota(shape, axis):
    return lax.broadcasted_iota(jnp.int32, shape, axis)


def waited(ref, sem):
    pltpu.make_async_copy(ref, ref, sem).wait()


def kernel(
    ids_col, ids_row, prob, cot_hbm, gate_hbm, up_hbm, w_gate, w_up, w_down,
    out, scores,
    cot, saved_gate, saved_up, in_sem,
    sent0, sent1, routed0, routed1, wd, wg, wu, a_sent, a_got, hidden, part, mate_part, total, back, handed,
    send_sem, routed_sem, relay_sem, w_send, w_sem, w_own, a_send, a_sem, h_send, h_sem,
    mate_send, mate_sem, total_send, back_sem, hand_send, hand_sem,
):
    sec = lax.axis_index("section")
    me = lax.axis_index("expert")
    sections = lax.axis_size("section")
    z, x = me // X, me % X
    expert, side = z // 2, z % 2
    mate = z + 1 - 2 * side
    mate_id = mate * X + x
    owned = jnp.where(side == 0, z + 1, Z - z)
    others = jnp.where(side == 0, Z - mate, mate + 1)
    away = jnp.where(side == 0, -1, 1)

    def at(index):
        return dict(device_id={"expert": index}, device_id_type=MESH)

    def band(plane):
        return pl.ds(pl.multiple_of(plane * BAND, BAND), BAND)

    def rows16(index):
        return pl.ds(pl.multiple_of(index * TILE, TILE), TILE)

    sent, routed = (sent0, sent1), (routed0, routed1)
    loads = [
        pltpu.make_async_copy(src, dst, in_sem.at[which])
        for which, (src, dst) in enumerate(((cot_hbm, cot), (gate_hbm, saved_gate), (up_hbm, saved_up)))
    ]
    for load in loads:
        load.start()
    barrier = pltpu.get_barrier_semaphore()

    def greet(step, carry):
        pl.semaphore_signal(barrier, inc=1, **at((me + step) % (X * Z)))
        return carry

    lax.fori_loop(1, X * Z, greet, 0)

    @pl.when(sec > 0)
    def _():
        pl.semaphore_signal(barrier, inc=1, device_id={"section": sec - 1}, device_id_type=MESH)

    @pl.when(sec < sections - 1)
    def _():
        pl.semaphore_signal(barrier, inc=1, device_id={"section": sec + 1}, device_id_type=MESH)

    ends = jnp.where(sec > 0, 1, 0) + jnp.where(sec < sections - 1, 1, 0)

    def pack():
        place = iota((TOK, 128), 0) % TILE
        folded = [jnp.zeros((TOK, 128), F32) for d in range(X)]
        for mb in range(2):
            ids = ids_row[mb]
            hot = (iota((8, TOK), 0) == ids).astype(F32)
            before = (iota((TOK, TOK), 0) < iota((TOK, TOK), 1)).astype(BF16)
            rank = jnp.sum(dot(hot.astype(BF16), before) * hot, axis=0, keepdims=True).astype(jnp.int32)
            row = iota((2 * TOK, TOK), 0)
            main = jnp.logical_and(row == ids * TILE + rank, jnp.logical_and(rank < TILE, row < TOK))
            last = jnp.logical_and((row - TOK) // TILE == ids, jnp.logical_and(rank == TILE, row >= TOK))
            pick = jnp.logical_or(main, last).astype(BF16)
            for d in range(X):
                picked = dot(pick, cot[mb, :, d * SLICE : (d + 1) * SLICE])
                sent[mb][d, :, 0:SLICE] = picked[0:TOK].astype(BF16)
                for k in range(CHUNKS):
                    folded[d] = jnp.where(
                        place == mb * 8 + k, picked[TOK:, k * 128 : (k + 1) * 128], folded[d]
                    )
        for d in range(X):
            sent0[d, :, SLICE:WIDE] = folded[d].astype(BF16)

    def dispatch(mb):
        def one(step, carry):
            far = step // X
            e = jnp.where(z < Z // 2, EXPERTS - 1 - far, far)
            d = (x + 1 + step) % X
            near = jnp.where(z <= 2 * e, 2 * e, 2 * e + 1)
            target = near * X + d
            src = sent[mb].at[d, rows16(e), :]
            dst = routed[mb].at[rows16(me), :]

            @pl.when(target == me)
            def _():
                pltpu.make_async_copy(src, dst, routed_sem.at[mb, z]).start()

            @pl.when(target != me)
            def _():
                pltpu.make_async_remote_copy(
                    src, dst, send_sem.at[mb], routed_sem.at[mb, z], **at(target)
                ).start()

            return carry

        lax.fori_loop(0, X * EXPERTS, one, 0)

    def relay(mb):
        def one(step, carry):
            plane = z + away * step
            block = routed[mb].at[band(plane), :]
            waited(block, routed_sem.at[mb, plane])
            pltpu.make_async_remote_copy(
                block, block, relay_sem.at[mb, plane], routed_sem.at[mb, plane], **at(mate_id)
            ).start()
            return carry

        lax.fori_loop(0, owned, one, 0)

    def arrivals(mb):
        def one(step, carry):
            plane = mate - away * step
            waited(routed[mb].at[band(plane), :], routed_sem.at[mb, plane])
            return carry

        lax.fori_loop(0, others, one, 0)

    def weights():
        for j in range(X):
            d = (x + j) % X
            across = pl.ds(pl.multiple_of(d * SLICE, 128), SLICE)
            pairs = (
                (w_down.at[:, across], wd.at[j]),
                (w_gate.at[across, :], wg.at[j]),
                (w_up.at[across, :], wu.at[j]),
            )
            for which, (src, dst) in enumerate(pairs):
                if j == 0:
                    pltpu.make_async_copy(src, dst, w_own.at[which]).start()
                else:
                    pltpu.make_async_remote_copy(
                        src, dst, w_send.at[which, j - 1], w_sem.at[which, j - 1], **at(z * X + d)
                    ).start()

    def weights_here(which, ref):
        waited(ref.at[0], w_own.at[which])
        for j in range(1, X):
            waited(ref.at[j], w_sem.at[which, j - 1])

    def first_product(mb):
        row = iota((CHUNKS * SOURCES, MAIN), 0)
        unfold = (iota((CHUNKS * SOURCES, MAIN), 1) == (row % SOURCES) * TILE + mb * 8 + row // SOURCES).astype(BF16)
        tail = dot(unfold, routed0[:, SLICE:WIDE]).astype(BF16)
        tail = jnp.concatenate(
            [tail[k * SOURCES : (k + 1) * SOURCES] for k in range(CHUNKS)], axis=1
        )
        for j in range(X):
            a_sent[mb, j, 0:MAIN] = dot_t(routed[mb][:, 0:SLICE], wd[j]).astype(BF16)
            a_sent[mb, j, MAIN:ROWS] = dot_t(tail, wd[j]).astype(BF16)
        for j in range(1, X):
            pltpu.make_async_remote_copy(
                a_sent.at[mb, j], a_got.at[mb, j - 1], a_send.at[mb, j - 1], a_sem.at[mb, j - 1],
                **at(z * X + (x + X - j) % X),
            ).start()

    def activate(mb):
        for j in range(1, X):
            waited(a_got.at[mb, j - 1], a_sem.at[mb, j - 1])
        a = a_sent[mb, 0].astype(F32)
        for j in range(1, X):
            a = a + a_got[mb, j - 1].astype(F32)
        g = saved_gate[mb].astype(F32)
        u = saved_up[mb].astype(F32)
        sg = 1.0 / (1.0 + jnp.exp(-g))
        grad_up = a * (g * sg)
        grad_gate = a * u * sg * (1.0 + g * (1.0 - sg))
        hidden[mb, 0, :, 0:FH] = grad_gate.astype(BF16)
        hidden[mb, 0, :, FH : 2 * FH] = grad_up.astype(BF16)
        for j in range(1, X):
            pltpu.make_async_remote_copy(
                hidden.at[mb, 0], hidden.at[mb, j], h_send.at[mb, j - 1], h_sem.at[mb, j - 1],
                **at(z * X + (x + j) % X),
            ).start()
        score = jnp.sum(grad_up * u, axis=1, keepdims=True)
        row = iota((ROWS, 128), 0)
        slot = jnp.where(row < MAIN, row % TILE, TILE)
        spread = jnp.where(iota((ROWS, 128), 1) == slot, score, 0.0).astype(BF16)
        row, other = iota((MAIN, ROWS), 0), iota((MAIN, ROWS), 1)
        source = jnp.where(other < MAIN, other // TILE, other - MAIN)
        gather = jnp.logical_and(row % TILE == SCORE_ROW, row // TILE == source).astype(BF16)
        part[mb, :, SLICE:WIDE] = dot(gather, spread).astype(BF16)

    def second_product(mb):
        for j in range(1, X):
            waited(hidden.at[mb, j], h_sem.at[mb, j - 1])
        grads = jnp.zeros((ROWS, SLICE), F32)
        for j in range(X):
            both = jnp.concatenate([wg[j], wu[j]], axis=1)
            grads = grads + dot_t(hidden[mb, j], both)
        part[mb, :, 0:SLICE] = grads[0:MAIN].astype(BF16)
        tail = grads[MAIN:ROWS].astype(BF16)
        spread = dot((iota((MAIN, SOURCES), 0) // TILE == iota((MAIN, SOURCES), 1)).astype(BF16), tail)
        place = iota((MAIN, 128), 0) % TILE
        folded = part[mb, :, SLICE:WIDE].astype(F32)
        for k in range(CHUNKS):
            folded = jnp.where(place == k, spread[:, k * 128 : (k + 1) * 128], folded)
        part[mb, :, SLICE:WIDE] = folded.astype(BF16)

    def send_back(mb, stage):
        def give(step, carry):
            plane = mate - away * (others - 1 - step)
            pltpu.make_async_remote_copy(
                part.at[mb, band(plane), :], mate_part.at[mb, band(plane), :],
                mate_send.at[mb, plane], mate_sem.at[mb, plane], **at(mate_id),
            ).start()
            return carry

        def take(step, carry):
            plane = z + away * (owned - 1 - step)
            rows = band(plane)
            waited(mate_part.at[mb, rows, :], mate_sem.at[mb, plane])
            both = part[mb, rows, :].astype(F32) + mate_part[mb, rows, :].astype(F32)
            total[mb, rows, :] = both.astype(BF16)

            def to(step, carry):
                target = plane * X + (x + 1 + step) % X
                src = total.at[mb, rows16(target), :]
                dst = back.at[mb, x, rows16(expert), :]

                @pl.when(target == me)
                def _():
                    pltpu.make_async_copy(src, dst, back_sem.at[mb]).start()

                @pl.when(target != me)
                def _():
                    pltpu.make_async_remote_copy(
                        src, dst, total_send.at[mb, plane], back_sem.at[mb], **at(target)
                    ).start()

                return carry

            lax.fori_loop(0, X, to, 0)
            return carry

        if stage == 0:
            lax.fori_loop(0, others, give, 0)
        else:
            lax.fori_loop(0, owned, take, 0)

    def finish(mb):
        waited(back.at[mb], back_sem.at[mb])
        ids = ids_col[mb]
        lane = iota((TOK, 128), 1)
        hot = (lane == ids).astype(F32)
        before = (iota((TOK, TOK), 1) < iota((TOK, TOK), 0)).astype(BF16)
        rank = jnp.sum(dot(before, hot.astype(BF16)) * hot, axis=1, keepdims=True).astype(jnp.int32)
        column = iota((TOK, TOK), 1)
        main = jnp.logical_and(column == ids * TILE + rank, rank < TILE).astype(BF16)
        group = [
            jnp.logical_and(column == ids * TILE + k, rank == TILE).astype(F32) for k in range(CHUNKS)
        ]
        group.append((column == ids * TILE + SCORE_ROW).astype(F32))
        pick = jnp.concatenate(group, axis=0).astype(BF16)
        score = jnp.zeros((TOK, 128), F32)
        weight = prob[mb]
        for d in range(X):
            tail = dot(pick, back[mb, d, :, SLICE:WIDE])
            score = score + tail[CHUNKS * TOK :]
            grads = dot(main, back[mb, d, :, 0:SLICE])
            grads = grads + jnp.concatenate(
                [tail[k * TOK : (k + 1) * TOK] for k in range(CHUNKS)], axis=1
            )
            across = slice(d * SLICE, (d + 1) * SLICE)
            dx = (cot[mb, :, across].astype(F32) + weight * grads).astype(BF16)
            if mb == 0:
                handed[:, across] = dx
            else:
                out[mb, :, across] = dx
        scores[mb] = jnp.sum(jnp.where(lane == rank, score, 0.0), axis=1, keepdims=True)

    loads[0].wait()
    pack()
    pl.semaphore_wait(barrier, X * Z - 1 + ends)
    dispatch(0)
    weights()
    relay(0)
    dispatch(1)
    arrivals(0)
    weights_here(0, wd)
    first_product(0)
    relay(1)
    loads[1].wait()
    loads[2].wait()
    activate(0)
    weights_here(1, wg)
    weights_here(2, wu)
    second_product(0)
    send_back(0, 0)
    arrivals(1)
    first_product(1)
    activate(1)
    send_back(0, 1)
    second_product(1)
    send_back(1, 0)
    send_back(1, 1)
    finish(0)

    @pl.when(sec > 0)
    def _():
        pltpu.make_async_remote_copy(
            handed, out.at[0], hand_send, hand_sem, device_id={"section": sec - 1}, device_id_type=MESH
        ).start()

    @pl.when(sec == sections - 1)
    def _():
        out[0] = jnp.zeros((TOK, D), BF16)

    finish(1)

    for mb in range(2):
        waited(routed[mb].at[pl.ds(0, (X * EXPERTS - 1) * TILE), :], send_sem.at[mb])

        def relayed(step, carry):
            plane = z + away * step
            waited(routed[mb].at[band(plane), :], relay_sem.at[mb, plane])
            rows = total.at[mb, band(plane), :]

            @pl.when(plane == z)
            def _():
                waited(total.at[mb, pl.ds(0, BAND - TILE), :], total_send.at[mb, plane])

            @pl.when(plane != z)
            def _():
                waited(rows, total_send.at[mb, plane])

            return carry

        lax.fori_loop(0, owned, relayed, 0)

        def mated(step, carry):
            plane = mate - away * step
            waited(part.at[mb, band(plane), :], mate_send.at[mb, plane])
            return carry

        lax.fori_loop(0, others, mated, 0)
        for j in range(1, X):
            waited(a_sent.at[mb, j], a_send.at[mb, j - 1])
            waited(hidden.at[mb, 0], h_send.at[mb, j - 1])
    for which, ref in enumerate((wd, wg, wu)):
        for j in range(1, X):
            waited(ref.at[j], w_send.at[which, j - 1])

    @pl.when(sec > 0)
    def _():
        waited(handed, hand_send)

    @pl.when(sec < sections - 1)
    def _():
        waited(out.at[0], hand_sem)


def on_device(cotangent, routes, gate_prob, saved_gate, saved_up, w_gate, w_up, w_down):
    def by_row(saved):
        main = saved[0, :, :, :TILE, :].reshape(2, MAIN, FH)
        return jnp.concatenate([main, saved[0, :, :, TILE, :]], axis=1)

    vmem = pl.BlockSpec(memory_space=pltpu.VMEM)
    hbm = pl.BlockSpec(memory_space=pltpu.HBM)
    dma = pltpu.SemaphoreType.DMA
    grads, scores = pl.pallas_call(
        kernel,
        out_shape=(
            jax.ShapeDtypeStruct((2, TOK, D), BF16),
            jax.ShapeDtypeStruct((2, TOK, 1), F32),
        ),
        in_specs=[vmem] * 3 + [hbm] * 6,
        out_specs=(vmem, vmem),
        scratch_shapes=[
            pltpu.VMEM((2, TOK, D), BF16),
            pltpu.VMEM((2, ROWS, FH), BF16),
            pltpu.VMEM((2, ROWS, FH), BF16),
            dma((3,)),
            pltpu.VMEM((X, TOK, WIDE), BF16),
            pltpu.VMEM((X, TOK, SLICE), BF16),
            pltpu.VMEM((MAIN, WIDE), BF16),
            pltpu.VMEM((MAIN, SLICE), BF16),
            pltpu.VMEM((X, FH, SLICE), BF16),
            pltpu.VMEM((X, SLICE, FH), BF16),
            pltpu.VMEM((X, SLICE, FH), BF16),
            pltpu.VMEM((2, X, ROWS, FH), BF16),
            pltpu.VMEM((2, X - 1, ROWS, FH), BF16),
            pltpu.VMEM((2, X, ROWS, 2 * FH), BF16),
            pltpu.VMEM((2, MAIN, WIDE), BF16),
            pltpu.VMEM((2, MAIN, WIDE), BF16),
            pltpu.VMEM((2, MAIN, WIDE), BF16),
            pltpu.VMEM((2, X, TOK, WIDE), BF16),
            pltpu.VMEM((TOK, D), BF16),
            dma((2,)),
            dma((2, Z)),
            dma((2, Z)),
            dma((3, X - 1)),
            dma((3, X - 1)),
            dma((3,)),
            dma((2, X - 1)),
            dma((2, X - 1)),
            dma((2, X - 1)),
            dma((2, X - 1)),
            dma((2, Z)),
            dma((2, Z)),
            dma((2, Z)),
            dma((2,)),
            dma,
            dma,
        ],
        compiler_params=pltpu.CompilerParams(
            collective_id=0, has_side_effects=True, vmem_limit_bytes=VMEM_MB * 1024 * 1024
        ),
        cost_estimate=pl.CostEstimate(
            flops=6 * 2 * ROWS * D * FH, bytes_accessed=8 * 1024 * 1024, transcendentals=2 * ROWS * FH
        ),
    )(
        routes[0],
        routes[0].reshape(2, 1, TOK),
        gate_prob[0],
        cotangent[0],
        by_row(saved_gate),
        by_row(saved_up),
        w_gate[0],
        w_up[0],
        w_down[0],
    )
    return grads[None], scores[None]


def solution(mesh):
    in_specs = (
        P("section", None, "expert", None),
        P("section", None, "expert", None),
        P("section", None, "expert", None),
        P("section", None, None, None, "expert"),
        P("section", None, None, None, "expert"),
        P("section", None, "expert"),
        P("section", None, "expert"),
        P("section", "expert", None),
    )
    out_specs = (P("section", None, "expert", None), P("section", None, "expert", None))
    return jax.shard_map(
        on_device, mesh=mesh, in_specs=in_specs, out_specs=out_specs, check_vma=False
    )
```

```python
import jax
import jax.numpy as jnp
from jax import lax
from jax.experimental import pallas as pl
from jax.experimental.pallas import tpu as pltpu
from jax.sharding import PartitionSpec as P

MESH = pl.DeviceIdType.MESH
BF16 = jnp.bfloat16
F32 = jnp.float32

TOK = 64
D = 3584
X = 4
Z = 8
EXPERTS = 4
SLICE = D // X
CHUNKS = SLICE // 128
TILE = 16
WIDE = SLICE + 128
SOURCES = X * Z
MAIN = SOURCES * TILE
ROWS = MAIN + SOURCES
FH = 128
BAND = X * TILE
VMEM_MB = 28
SCORE_ROW = 8


def dot(a, b):
    return lax.dot_general(a, b, (((1,), (0,)), ((), ())), preferred_element_type=F32)


def dot_t(a, b):
    return lax.dot_general(a, b, (((1,), (1,)), ((), ())), preferred_element_type=F32)


def iota(shape, axis):
    return lax.broadcasted_iota(jnp.int32, shape, axis)


def waited(ref, sem):
    pltpu.make_async_copy(ref, ref, sem).wait()


def kernel(
    ids_row, prob, cot_hbm, gate_hbm, up_hbm, w_gate, w_up, w_down,
    out, scores,
    cot, saved_gate, saved_up, in_sem,
    sent0, sent1, routed0, routed1, wd, wg, wu, a_sent, a_got, hidden, part, mate_part, total, back, handed,
    send_sem, routed_sem, relay_sem, w_send, w_sem, w_own, a_send, a_sem, h_send, h_sem,
    mate_send, mate_sem, total_send, back_sem, hand_send, hand_sem,
):
    sec = lax.axis_index("section")
    me = lax.axis_index("expert")
    sections = lax.axis_size("section")
    z, x = me // X, me % X
    expert, side = z // 2, z % 2
    mate = z + 1 - 2 * side
    mate_id = mate * X + x
    owned = jnp.where(side == 0, z + 1, Z - z)
    others = jnp.where(side == 0, Z - mate, mate + 1)
    away = jnp.where(side == 0, -1, 1)

    def at(index):
        return dict(device_id={"expert": index}, device_id_type=MESH)

    def band(plane):
        return pl.ds(pl.multiple_of(plane * BAND, BAND), BAND)

    def rows16(index):
        return pl.ds(pl.multiple_of(index * TILE, TILE), TILE)

    sent, routed = (sent0, sent1), (routed0, routed1)
    loads = [
        pltpu.make_async_copy(src, dst, in_sem.at[which])
        for which, (src, dst) in enumerate(((cot_hbm, cot), (gate_hbm, saved_gate), (up_hbm, saved_up)))
    ]
    for load in loads:
        load.start()
    barrier = pltpu.get_barrier_semaphore()

    def greet(step, carry):
        pl.semaphore_signal(barrier, inc=1, **at((me + step) % (X * Z)))
        return carry

    lax.fori_loop(1, X * Z, greet, 0)

    @pl.when(sec > 0)
    def _():
        pl.semaphore_signal(barrier, inc=1, device_id={"section": sec - 1}, device_id_type=MESH)

    @pl.when(sec < sections - 1)
    def _():
        pl.semaphore_signal(barrier, inc=1, device_id={"section": sec + 1}, device_id_type=MESH)

    ends = jnp.where(sec > 0, 1, 0) + jnp.where(sec < sections - 1, 1, 0)

    def pack():
        place = iota((TOK, 128), 0) % TILE
        folded = [jnp.zeros((TOK, 128), F32) for d in range(X)]
        for mb in range(2):
            ids = ids_row[mb]
            hot = (iota((8, TOK), 0) == ids).astype(F32)
            before = (iota((TOK, TOK), 0) < iota((TOK, TOK), 1)).astype(BF16)
            rank = jnp.sum(dot(hot.astype(BF16), before) * hot, axis=0, keepdims=True).astype(jnp.int32)
            row = iota((2 * TOK, TOK), 0)
            main = jnp.logical_and(row == ids * TILE + rank, jnp.logical_and(rank < TILE, row < TOK))
            last = jnp.logical_and((row - TOK) // TILE == ids, jnp.logical_and(rank == TILE, row >= TOK))
            pick = jnp.logical_or(main, last).astype(BF16)
            for d in range(X):
                picked = dot(pick, cot[mb, :, d * SLICE : (d + 1) * SLICE])
                sent[mb][d, :, 0:SLICE] = picked[0:TOK].astype(BF16)
                for k in range(CHUNKS):
                    folded[d] = jnp.where(
                        place == mb * 8 + k, picked[TOK:, k * 128 : (k + 1) * 128], folded[d]
                    )
        for d in range(X):
            sent0[d, :, SLICE:WIDE] = folded[d].astype(BF16)

    def dispatch(mb, turn):
        def one(step, carry):
            e = jnp.where(z < Z // 2, EXPERTS - 1 - step, step)
            d = (x + 1 + turn) % X
            near = jnp.where(z <= 2 * e, 2 * e, 2 * e + 1)
            target = near * X + d
            src = sent[mb].at[d, rows16(e), :]
            dst = routed[mb].at[rows16(me), :]

            @pl.when(target == me)
            def _():
                pltpu.make_async_copy(src, dst, routed_sem.at[mb, me]).start()

            @pl.when(target != me)
            def _():
                pltpu.make_async_remote_copy(
                    src, dst, send_sem.at[mb], routed_sem.at[mb, me], **at(target)
                ).start()

            return carry

        lax.fori_loop(0, EXPERTS, one, 0)

    def relay(mb, turn):
        def one(step, carry):
            source = (z + away * step) * X + (x + X - 1 - turn) % X
            block = routed[mb].at[rows16(source), :]
            waited(block, routed_sem.at[mb, source])
            pltpu.make_async_remote_copy(
                block, block, relay_sem.at[mb, source], routed_sem.at[mb, source], **at(mate_id)
            ).start()
            return carry

        lax.fori_loop(0, owned, one, 0)

    def arrivals(mb):
        def one(step, carry):
            source = (mate - away * (step // X)) * X + step % X
            waited(routed[mb].at[rows16(source), :], routed_sem.at[mb, source])
            return carry

        lax.fori_loop(0, X * others, one, 0)

    def weights(wanted):
        for j in range(X):
            d = (x + j) % X
            across = pl.ds(pl.multiple_of(d * SLICE, 128), SLICE)
            pairs = (
                (w_down.at[:, across], wd.at[j]),
                (w_gate.at[across, :], wg.at[j]),
                (w_up.at[across, :], wu.at[j]),
            )
            for which, (src, dst) in enumerate(pairs):
                if which not in wanted:
                    continue
                if j == 0:
                    pltpu.make_async_copy(src, dst, w_own.at[which]).start()
                else:
                    pltpu.make_async_remote_copy(
                        src, dst, w_send.at[which, j - 1], w_sem.at[which, j - 1], **at(z * X + d)
                    ).start()

    def weights_here(which, ref):
        waited(ref.at[0], w_own.at[which])
        for j in range(1, X):
            waited(ref.at[j], w_sem.at[which, j - 1])

    def first_product(mb):
        row = iota((CHUNKS * SOURCES, MAIN), 0)
        unfold = (iota((CHUNKS * SOURCES, MAIN), 1) == (row % SOURCES) * TILE + mb * 8 + row // SOURCES).astype(BF16)
        tail = dot(unfold, routed0[:, SLICE:WIDE]).astype(BF16)
        tail = jnp.concatenate(
            [tail[k * SOURCES : (k + 1) * SOURCES] for k in range(CHUNKS)], axis=1
        )
        for j in range(X):
            a_sent[mb, j, 0:MAIN] = dot_t(routed[mb][:, 0:SLICE], wd[j]).astype(BF16)
            a_sent[mb, j, MAIN:ROWS] = dot_t(tail, wd[j]).astype(BF16)
        for j in range(1, X):
            pltpu.make_async_remote_copy(
                a_sent.at[mb, j], a_got.at[mb, j - 1], a_send.at[mb, j - 1], a_sem.at[mb, j - 1],
                **at(z * X + (x + X - j) % X),
            ).start()

    def activate(mb):
        for j in range(1, X):
            waited(a_got.at[mb, j - 1], a_sem.at[mb, j - 1])
        a = a_sent[mb, 0].astype(F32)
        for j in range(1, X):
            a = a + a_got[mb, j - 1].astype(F32)
        g = saved_gate[mb].astype(F32)
        u = saved_up[mb].astype(F32)
        sg = 1.0 / (1.0 + jnp.exp(-g))
        grad_up = a * (g * sg)
        grad_gate = a * u * sg * (1.0 + g * (1.0 - sg))
        hidden[mb, 0, :, 0:FH] = grad_gate.astype(BF16)
        hidden[mb, 0, :, FH : 2 * FH] = grad_up.astype(BF16)
        for j in range(1, X):
            pltpu.make_async_remote_copy(
                hidden.at[mb, 0], hidden.at[mb, j], h_send.at[mb, j - 1], h_sem.at[mb, j - 1],
                **at(z * X + (x + j) % X),
            ).start()
        score = jnp.sum(grad_up * u, axis=1, keepdims=True)
        row = iota((ROWS, 128), 0)
        slot = jnp.where(row < MAIN, row % TILE, TILE)
        spread = jnp.where(iota((ROWS, 128), 1) == slot, score, 0.0).astype(BF16)
        row, other = iota((MAIN, ROWS), 0), iota((MAIN, ROWS), 1)
        source = jnp.where(other < MAIN, other // TILE, other - MAIN)
        gather = jnp.logical_and(row % TILE == SCORE_ROW, row // TILE == source).astype(BF16)
        part[mb, :, SLICE:WIDE] = dot(gather, spread).astype(BF16)

    def second_product(mb):
        for j in range(1, X):
            waited(hidden.at[mb, j], h_sem.at[mb, j - 1])
        grads = jnp.zeros((ROWS, SLICE), F32)
        for j in range(X):
            both = jnp.concatenate([wg[j], wu[j]], axis=1)
            grads = grads + dot_t(hidden[mb, j], both)
        part[mb, :, 0:SLICE] = grads[0:MAIN].astype(BF16)
        tail = grads[MAIN:ROWS].astype(BF16)
        spread = dot((iota((MAIN, SOURCES), 0) // TILE == iota((MAIN, SOURCES), 1)).astype(BF16), tail)
        place = iota((MAIN, 128), 0) % TILE
        folded = part[mb, :, SLICE:WIDE].astype(F32)
        for k in range(CHUNKS):
            folded = jnp.where(place == k, spread[:, k * 128 : (k + 1) * 128], folded)
        part[mb, :, SLICE:WIDE] = folded.astype(BF16)

    def send_back(mb, stage):
        def give(step, carry):
            plane = mate - away * (others - 1 - step)
            pltpu.make_async_remote_copy(
                part.at[mb, band(plane), :], mate_part.at[mb, band(plane), :],
                mate_send.at[mb, plane], mate_sem.at[mb, plane], **at(mate_id),
            ).start()
            return carry

        def take(step, carry):
            plane = z + away * (owned - 1 - step)
            rows = band(plane)
            waited(mate_part.at[mb, rows, :], mate_sem.at[mb, plane])
            both = part[mb, rows, :].astype(F32) + mate_part[mb, rows, :].astype(F32)
            total[mb, rows, :] = both.astype(BF16)

            def to(step, carry):
                target = plane * X + (x + 1 + step) % X
                src = total.at[mb, rows16(target), :]
                dst = back.at[mb, x, rows16(expert), :]

                @pl.when(target == me)
                def _():
                    pltpu.make_async_copy(src, dst, back_sem.at[mb]).start()

                @pl.when(target != me)
                def _():
                    pltpu.make_async_remote_copy(
                        src, dst, total_send.at[mb, plane], back_sem.at[mb], **at(target)
                    ).start()

                return carry

            lax.fori_loop(0, X, to, 0)
            return carry

        if stage == 0:
            lax.fori_loop(0, others, give, 0)
        else:
            lax.fori_loop(0, owned, take, 0)

    def finish(mb):
        waited(back.at[mb], back_sem.at[mb])
        same = iota((TOK, TOK), 0) == iota((TOK, TOK), 1)

        def upright(row):
            return jnp.sum(jnp.where(same, row, 0.0), axis=1, keepdims=True)

        ids = upright(ids_row[mb].astype(F32)).astype(jnp.int32)
        lane = iota((TOK, 128), 1)
        hot = (lane == ids).astype(F32)
        before = (iota((TOK, TOK), 1) < iota((TOK, TOK), 0)).astype(BF16)
        rank = jnp.sum(dot(before, hot.astype(BF16)) * hot, axis=1, keepdims=True).astype(jnp.int32)
        column = iota((TOK, TOK), 1)
        main = jnp.logical_and(column == ids * TILE + rank, rank < TILE).astype(BF16)
        group = [
            jnp.logical_and(column == ids * TILE + k, rank == TILE).astype(F32) for k in range(CHUNKS)
        ]
        group.append((column == ids * TILE + SCORE_ROW).astype(F32))
        pick = jnp.concatenate(group, axis=0).astype(BF16)
        score = jnp.zeros((TOK, 128), F32)
        weight = upright(prob[mb])
        for d in range(X):
            tail = dot(pick, back[mb, d, :, SLICE:WIDE])
            score = score + tail[CHUNKS * TOK :]
            grads = dot(main, back[mb, d, :, 0:SLICE])
            grads = grads + jnp.concatenate(
                [tail[k * TOK : (k + 1) * TOK] for k in range(CHUNKS)], axis=1
            )
            across = slice(d * SLICE, (d + 1) * SLICE)
            dx = (cot[mb, :, across].astype(F32) + weight * grads).astype(BF16)
            if mb == 0:
                handed[:, across] = dx
            else:
                out[mb, :, across] = dx
        score = jnp.sum(jnp.where(lane == rank, score, 0.0), axis=1, keepdims=True)
        scores[mb] = jnp.sum(jnp.where(same, score, 0.0), axis=0, keepdims=True)

    loads[0].wait()
    pack()
    pl.semaphore_wait(barrier, X * Z - 1 + ends)
    for turn in range(X):
        dispatch(0, turn)
    weights((0,))
    weights((1, 2))
    for turn in range(X):
        relay(0, turn)
    for turn in range(X):
        dispatch(1, turn)
    arrivals(0)
    weights_here(0, wd)
    first_product(0)
    for turn in range(X):
        relay(1, turn)
    loads[1].wait()
    loads[2].wait()
    activate(0)
    weights_here(1, wg)
    weights_here(2, wu)
    second_product(0)
    send_back(0, 0)
    arrivals(1)
    first_product(1)
    activate(1)
    send_back(0, 1)
    second_product(1)
    send_back(1, 0)
    send_back(1, 1)
    finish(0)

    @pl.when(sec > 0)
    def _():
        pltpu.make_async_remote_copy(
            handed, out.at[0], hand_send, hand_sem, device_id={"section": sec - 1}, device_id_type=MESH
        ).start()

    @pl.when(sec == sections - 1)
    def _():
        out[0] = jnp.zeros((TOK, D), BF16)

    finish(1)

    for mb in range(2):
        waited(routed[mb].at[pl.ds(0, (X * EXPERTS - 1) * TILE), :], send_sem.at[mb])

        def relayed(step, carry):
            plane = z + away * step
            for other in range(X):
                source = plane * X + other
                waited(routed[mb].at[rows16(source), :], relay_sem.at[mb, source])
            rows = total.at[mb, band(plane), :]

            @pl.when(plane == z)
            def _():
                waited(total.at[mb, pl.ds(0, BAND - TILE), :], total_send.at[mb, plane])

            @pl.when(plane != z)
            def _():
                waited(rows, total_send.at[mb, plane])

            return carry

        lax.fori_loop(0, owned, relayed, 0)

        def mated(step, carry):
            plane = mate - away * step
            waited(part.at[mb, band(plane), :], mate_send.at[mb, plane])
            return carry

        lax.fori_loop(0, others, mated, 0)
        for j in range(1, X):
            waited(a_sent.at[mb, j], a_send.at[mb, j - 1])
            waited(hidden.at[mb, 0], h_send.at[mb, j - 1])
    for which, ref in enumerate((wd, wg, wu)):
        for j in range(1, X):
            waited(ref.at[j], w_send.at[which, j - 1])

    @pl.when(sec > 0)
    def _():
        waited(handed, hand_send)

    @pl.when(sec < sections - 1)
    def _():
        waited(out.at[0], hand_sem)


def on_device(cotangent, routes, gate_prob, saved_gate, saved_up, w_gate, w_up, w_down):
    def by_row(saved):
        main = saved[0, :, :, :TILE, :].reshape(2, MAIN, FH)
        return jnp.concatenate([main, saved[0, :, :, TILE, :]], axis=1)

    vmem = pl.BlockSpec(memory_space=pltpu.VMEM)
    hbm = pl.BlockSpec(memory_space=pltpu.HBM)
    dma = pltpu.SemaphoreType.DMA
    grads, scores = pl.pallas_call(
        kernel,
        out_shape=(
            jax.ShapeDtypeStruct((2, TOK, D), BF16),
            jax.ShapeDtypeStruct((2, 1, TOK), F32),
        ),
        in_specs=[vmem] * 2 + [hbm] * 6,
        out_specs=(vmem, vmem),
        scratch_shapes=[
            pltpu.VMEM((2, TOK, D), BF16),
            pltpu.VMEM((2, ROWS, FH), BF16),
            pltpu.VMEM((2, ROWS, FH), BF16),
            dma((3,)),
            pltpu.VMEM((X, TOK, WIDE), BF16),
            pltpu.VMEM((X, TOK, SLICE), BF16),
            pltpu.VMEM((MAIN, WIDE), BF16),
            pltpu.VMEM((MAIN, SLICE), BF16),
            pltpu.VMEM((X, FH, SLICE), BF16),
            pltpu.VMEM((X, SLICE, FH), BF16),
            pltpu.VMEM((X, SLICE, FH), BF16),
            pltpu.VMEM((2, X, ROWS, FH), BF16),
            pltpu.VMEM((2, X - 1, ROWS, FH), BF16),
            pltpu.VMEM((2, X, ROWS, 2 * FH), BF16),
            pltpu.VMEM((2, MAIN, WIDE), BF16),
            pltpu.VMEM((2, MAIN, WIDE), BF16),
            pltpu.VMEM((2, MAIN, WIDE), BF16),
            pltpu.VMEM((2, X, TOK, WIDE), BF16),
            pltpu.VMEM((TOK, D), BF16),
            dma((2,)),
            dma((2, SOURCES)),
            dma((2, SOURCES)),
            dma((3, X - 1)),
            dma((3, X - 1)),
            dma((3,)),
            dma((2, X - 1)),
            dma((2, X - 1)),
            dma((2, X - 1)),
            dma((2, X - 1)),
            dma((2, Z)),
            dma((2, Z)),
            dma((2, Z)),
            dma((2,)),
            dma,
            dma,
        ],
        compiler_params=pltpu.CompilerParams(
            collective_id=0, has_side_effects=True, vmem_limit_bytes=VMEM_MB * 1024 * 1024
        ),
        cost_estimate=pl.CostEstimate(
            flops=6 * 2 * ROWS * D * FH, bytes_accessed=8 * 1024 * 1024, transcendentals=2 * ROWS * FH
        ),
    )(
        routes[0].reshape(2, 1, TOK),
        gate_prob[0].reshape(2, 1, TOK),
        cotangent[0],
        by_row(saved_gate),
        by_row(saved_up),
        w_gate[0],
        w_up[0],
        w_down[0],
    )
    return grads[None], scores.reshape(1, 2, TOK, 1)


def solution(mesh):
    in_specs = (
        P("section", None, "expert", None),
        P("section", None, "expert", None),
        P("section", None, "expert", None),
        P("section", None, None, None, "expert"),
        P("section", None, None, None, "expert"),
        P("section", None, "expert"),
        P("section", None, "expert"),
        P("section", "expert", None),
    )
    out_specs = (P("section", None, "expert", None), P("section", None, "expert", None))
    return jax.shard_map(
        on_device, mesh=mesh, in_specs=in_specs, out_specs=out_specs, check_vma=False
    )
```
